128 devices in a mesh: seq: 8 (over x, y_lo), rep: 16 (over z, y_hi, core).
Axes of the slice: x: 4, y: 4 (y_hi: 2, y_lo: 2; y = y_hi * 2 + y_lo), z: 4, core: 2. Of those that a mesh axis runs over, the one named last changes fastest.
Arguments:
- activations: bfloat16 [16, 1024, 2048], P('rep', 'seq'), may hold values from -6 to 6
- gate_values: bfloat16 [16, 1024, 2048], P('rep', 'seq'), may hold values from -6 to 6
- in_weight: bfloat16 [2048, 2048], P(('seq', 'rep')), may hold values from -0.125 to 0.125
- long_filter: bfloat16 [1024, 2048], P('seq'), may hold values from -0.1875 to 0.1875
- out_cotangent: bfloat16 [16, 1024, 2048], P('rep', 'seq'), may hold values from -6 to 6
Outputs:
- mixed_out: bfloat16 [16, 1024, 2048], P('rep', 'seq')
- gate_grad: bfloat16 [16, 1024, 2048], P('rep', 'seq')
- input_grad: bfloat16 [16, 1024, 2048], P('rep', 'seq')
- weight_grad: float32 [2048, 2048], P(('seq', 'rep'))
- filter_grad: float32 [1024, 2048], P(('seq', 'rep'))
The draws below stay inside these ranges and needn't reach their ends.
All inputs are finite; a program needn't handle non-finite values.
Results may differ from the reference program's by a relative error of at most 0.018.
Values may be sent and summed in bfloat16 or wider, within the bound.
No kernel may reach another device: no remote copies, remote signals or barrier semaphores. Data moves between devices by JAX's collectives and lax.ppermute only.
A program may use at most 256 MiB of HBM per device.

```python
import math
import jax
import jax.numpy as jnp
from jax import lax

D = 2048
C = 2048
LEN = 1024
REPS = 16


def spiked(result, stream_key, source, target, parts, factor):
    def block_of(position):
        return (jnp.arange(result.shape[position]) // (result.shape[position] // parts)).reshape((-1,) + (1,) * (result.ndim - 1 - position))

    near = jax.random.permutation(stream_key, parts)[block_of(target)]
    second = (block_of(target) + parts // 2) % parts
    return jnp.where((block_of(source) == near) | (block_of(source) == second), factor * result, result)


def shard_levels(key, dims, cuts, least, high):
    factor_of = 1.0
    for position, parts in cuts:
        steps = jax.random.uniform(jax.random.fold_in(jax.random.fold_in(key, 6), position), (parts,), jnp.float32, least / len(cuts), high / len(cuts))
        factor_of = factor_of * jnp.repeat(jnp.exp(steps), dims[position] // parts).reshape((-1,) + (1,) * (len(dims) - 1 - position))
    return factor_of


def centred(stream_key, shape, width, most, cuts=(), kind=jnp.bfloat16):
    level = shard_levels(stream_key, shape, cuts, -0.22, 0.18) if cuts else 1.0
    values = jax.random.normal(stream_key, shape, jnp.float32) * width * level
    return jnp.minimum(jnp.maximum(values, -most), most).astype(kind)


def bell_draw_with(key, dims, width, limit, shards, heavy, dtype=jnp.bfloat16):
    result = width * jax.random.normal(key, dims, jnp.float32)
    if shards:
        result = result * shard_levels(key, dims, shards, -0.22, 0.18)
    return jnp.clip(spiked(result, jax.random.fold_in(key, 3), *heavy), -limit, limit).astype(dtype)


def setup_inputs(seed: int = 0) -> dict:
    key_list = jax.random.split(jax.random.key(seed), 6)
    return {
        "activations": bell_draw_with(key_list[0], (REPS, LEN, D), 1.0, 6.0, ((0, 16), (1, 8)), (1, 2, 8, 2.0)),
        "gate_values": centred(key_list[1], (REPS, LEN, C), 1.0, 6.0, ((0, 16), (1, 8))),
        "in_weight": centred(key_list[2], (D, C), D ** -0.5, 0.125, ((0, 128),)),
        "long_filter": centred(key_list[3], (LEN, C), LEN ** -0.5, 0.1875, ((0, 8),)),
        "out_cotangent": centred(key_list[4], (REPS, LEN, C), 1.0, 6.0, ((0, 16), (1, 8))),
    }


def reference(activations, gate_values, in_weight, long_filter, out_cotangent):
    length = 2 * LEN
    filter_spectrum = jnp.fft.rfft(long_filter.astype(jnp.float32), n=length, axis=0)
    scale = 1.0 / math.sqrt(LEN * REPS)

    def one_sequence(carry, item):
        tokens, gates, upstream = item
        values = jnp.dot(tokens, in_weight, preferred_element_type=jnp.float32).astype(jnp.bfloat16)
        value_spectrum = jnp.fft.rfft(values.astype(jnp.float32), n=length, axis=0)
        conv = jnp.fft.irfft(value_spectrum * filter_spectrum, n=length, axis=0)[:LEN]
        gates_f = gates.astype(jnp.float32)
        upstream_f = upstream.astype(jnp.float32)
        mixed = (gates_f * conv).astype(jnp.bfloat16)
        gate_grad = (upstream_f * conv).astype(jnp.bfloat16)
        inner = (upstream_f * gates_f).astype(jnp.bfloat16)
        inner_spectrum = jnp.fft.rfft(inner.astype(jnp.float32), n=length, axis=0)
        value_grad = jnp.fft.irfft(jnp.conj(filter_spectrum) * inner_spectrum, n=length, axis=0)[:LEN]
        value_grad = value_grad.astype(jnp.bfloat16)
        input_grad = jnp.dot(value_grad, in_weight.T, preferred_element_type=jnp.float32).astype(jnp.bfloat16)
        weight_term = jnp.dot(tokens.T, value_grad, preferred_element_type=jnp.float32)
        filter_term = jnp.fft.irfft(inner_spectrum * jnp.conj(value_spectrum), n=length, axis=0)[:LEN]
        return ((carry[0] + weight_term, carry[1] + filter_term), (mixed, gate_grad, input_grad))
    start = (jnp.zeros((D, C), jnp.float32), jnp.zeros((LEN, C), jnp.float32))
    totals, outputs = lax.scan(one_sequence, start, (activations, gate_values, out_cotangent))
    return (outputs[0], outputs[1], outputs[2], totals[0] * scale, totals[1] * scale)
```

```python
import math

import jax
import jax.numpy as jnp
import numpy as np
from jax import lax
from jax.sharding import PartitionSpec as P

F32 = jnp.float32
BF16 = jnp.bfloat16


def tables(length):
    odd = 2 * np.arange(length, dtype=np.int64)[:, None] + 1
    phase = odd * np.arange(length, dtype=np.int64)[None, :] % (4 * length)
    angle = phase.astype(np.float64) * (math.pi / (2 * length))
    return (np.cos(angle), np.sin(angle))


def dot(a, b, dims=((1,), (0,))):
    return lax.dot_general(a, b, (dims, ((), ())), preferred_element_type=F32)


def local(activations, gate_values, in_weight, long_filter, out_cotangent):
    tokens = activations[0]
    gates = gate_values[0].astype(F32)
    upstream = out_cotangent[0].astype(F32)
    groups = lax.axis_size("seq")
    replicas = lax.axis_size("rep")
    block, channels = gates.shape
    features = tokens.shape[1]
    length = block * groups
    part = channels // groups
    rows = in_weight.shape[0]

    cosine, sine = tables(length)
    cos_t = jnp.asarray(cosine.astype(np.float32)).astype(BF16)
    sin_t = jnp.asarray(sine.astype(np.float32)).astype(BF16)

    def to_channels(x):
        return lax.all_to_all(x, "seq", 1, 0, tiled=True)

    def to_tokens(x):
        return lax.all_to_all(x, "seq", 0, 1, tiled=True)

    def spectrum(x):
        return (dot(cos_t, x), dot(sin_t, x))

    def inverse(real, imag):
        return (
            dot(cos_t, real.astype(BF16), ((0,), (0,))) + dot(sin_t, imag.astype(BF16), ((0,), (0,)))
        ) * (1.0 / length)

    inner = to_channels((upstream * gates).astype(BF16))
    taps = to_channels(long_filter)
    acts = lax.all_gather(tokens, "seq", axis=0, tiled=True)
    piece = to_channels(in_weight)
    weight = lax.all_gather(piece, "rep", axis=0, tiled=True)
    weight = weight.reshape(replicas, groups, rows, part).transpose(1, 0, 2, 3).reshape(features, part)

    f_c, f_s = spectrum(taps)
    i_c, i_s = spectrum(inner)
    value_grad = inverse(f_c * i_c + f_s * i_s, f_c * i_s - f_s * i_c).astype(BF16)

    values = dot(acts, weight).astype(BF16)
    v_c, v_s = spectrum(values)
    conv = inverse(f_c * v_c - f_s * v_s, f_c * v_s + f_s * v_c)
    conv = to_tokens(conv.astype(BF16)).astype(F32)
    mixed_out = (gates * conv).astype(BF16)
    gate_grad = (upstream * conv).astype(BF16)

    scale = 1.0 / math.sqrt(length * replicas)
    filter_part = inverse(v_c * i_c + v_s * i_s, v_c * i_s - v_s * i_c) * scale

    partial = dot(value_grad, weight, ((1,), (1,)))
    input_grad = lax.psum_scatter(partial.astype(BF16), "seq", scatter_dimension=0, tiled=True)

    weight_part = dot(acts, value_grad, ((0,), (0,))) * scale

    def reduce_rows(x):
        x = x.reshape(groups, replicas, -1, part).transpose(1, 0, 2, 3).reshape(-1, part)
        x = lax.psum_scatter(x, "rep", scatter_dimension=0, tiled=True)
        return lax.all_to_all(x, "seq", 0, 1, tiled=True)

    weight_grad = reduce_rows(weight_part)
    filter_grad = reduce_rows(filter_part)
    return (mixed_out[None], gate_grad[None], input_grad[None], weight_grad, filter_grad)


def solution(mesh):
    in_specs = (
        P("rep", "seq", None),
        P("rep", "seq", None),
        P(("seq", "rep"), None),
        P("seq", None),
        P("rep", "seq", None),
    )
    out_specs = (
        P("rep", "seq", None),
        P("rep", "seq", None),
        P("rep", "seq", None),
        P(("seq", "rep"), None),
        P(("seq", "rep"), None),
    )
    return jax.shard_map(local, mesh=mesh, in_specs=in_specs, out_specs=out_specs, check_vma=False)
```

```python
import math

import jax
import jax.numpy as jnp
import numpy as np
from jax import lax
from jax.sharding import PartitionSpec as P

F32 = jnp.float32
BF16 = jnp.bfloat16


def tables(length):
    odd = 2 * np.arange(length, dtype=np.int64)[:, None] + 1
    phase = odd * np.arange(length, dtype=np.int64)[None, :] % (4 * length)
    angle = phase.astype(np.float64) * (math.pi / (2 * length))
    return (np.cos(angle), np.sin(angle))


def dot(a, b, dims=((1,), (0,))):
    return lax.dot_general(a, b, (dims, ((), ())), preferred_element_type=F32)


def local(activations, gate_values, in_weight, long_filter, out_cotangent):
    tokens = activations[0]
    gates = gate_values[0].astype(F32)
    upstream = out_cotangent[0].astype(F32)
    groups = lax.axis_size("seq")
    replicas = lax.axis_size("rep")
    block, channels = gates.shape
    features = tokens.shape[1]
    length = block * groups
    part = channels // groups
    rows = in_weight.shape[0]

    cosine, sine = tables(length)
    cos_t = jnp.asarray(cosine.astype(np.float32)).astype(BF16)
    sin_t = jnp.asarray(sine.astype(np.float32)).astype(BF16)

    def to_channels(x):
        x = x.reshape(x.shape[0], groups, part).transpose(1, 0, 2)
        return lax.all_to_all(x, "seq", 0, 0, tiled=True)

    def to_tokens(x):
        return lax.all_to_all(x, "seq", 0, 1, tiled=True)

    def spectrum(x):
        return (dot(cos_t, x), dot(sin_t, x))

    def inverse(real, imag):
        return (
            dot(cos_t, real.astype(BF16), ((0,), (0,))) + dot(sin_t, imag.astype(BF16), ((0,), (0,)))
        ) * (1.0 / length)

    inner = (upstream * gates).astype(BF16)
    slices = to_channels(jnp.concatenate([inner, long_filter, in_weight], axis=0))
    inner = slices[:, :block].reshape(length, part)
    taps = slices[:, block : 2 * block].reshape(length, part)
    piece = slices[:, 2 * block :].reshape(groups * rows, part)
    acts = jnp.broadcast_to(tokens, (groups, block, features))
    acts = lax.all_to_all(acts, "seq", 0, 0, tiled=True).reshape(length, features)
    weight = lax.all_gather(piece, "rep", axis=0, tiled=True)
    weight = weight.reshape(replicas, groups, rows, part).transpose(1, 0, 2, 3).reshape(features, part)

    f_c, f_s = spectrum(taps)
    i_c, i_s = spectrum(inner)
    value_grad = inverse(f_c * i_c + f_s * i_s, f_c * i_s - f_s * i_c).astype(BF16)

    values = dot(acts, weight).astype(BF16)
    v_c, v_s = spectrum(values)
    conv = inverse(f_c * v_c - f_s * v_s, f_c * v_s + f_s * v_c)
    conv = to_tokens(conv.astype(BF16)).astype(F32)
    mixed_out = (gates * conv).astype(BF16)
    gate_grad = (upstream * conv).astype(BF16)

    scale = 1.0 / math.sqrt(length * replicas)
    filter_part = inverse(v_c * i_c + v_s * i_s, v_c * i_s - v_s * i_c) * scale

    partial = dot(value_grad, weight, ((1,), (1,)))
    input_grad = lax.psum_scatter(partial.astype(BF16), "seq", scatter_dimension=0, tiled=True)

    weight_part = dot(acts, value_grad, ((0,), (0,))) * scale

    owned = jnp.concatenate(
        [
            weight_part.astype(BF16).reshape(groups, replicas, -1, part),
            filter_part.astype(BF16).reshape(groups, replicas, -1, part),
        ],
        axis=2,
    )
    owned = lax.all_to_all(owned.transpose(1, 0, 2, 3), "rep", 0, 0, tiled=True)
    owned = jnp.sum(owned.astype(F32), axis=0)
    owned = lax.all_to_all(owned, "seq", 0, 0, tiled=True).transpose(1, 0, 2).reshape(-1, channels)
    weight_grad = owned[:rows]
    filter_grad = owned[rows:]
    return (mixed_out[None], gate_grad[None], input_grad[None], weight_grad, filter_grad)


def solution(mesh):
    in_specs = (
        P("rep", "seq", None),
        P("rep", "seq", None),
        P(("seq", "rep"), None),
        P("seq", None),
        P("rep", "seq", None),
    )
    out_specs = (
        P("rep", "seq", None),
        P("rep", "seq", None),
        P("rep", "seq", None),
        P(("seq", "rep"), None),
        P(("seq", "rep"), None),
    )
    return jax.shard_map(local, mesh=mesh, in_specs=in_specs, out_specs=out_specs, check_vma=False)
```

```python
import math

import jax
import jax.numpy as jnp
import numpy as np
from jax import lax
from jax.sharding import Mesh
from jax.sharding import PartitionSpec as P

F32 = jnp.float32
BF16 = jnp.bfloat16
SEQ = ("x", "yl")
REP = ("z", "yh", "core")
X, YL, Z, YH, CORE = 4, 2, 4, 2, 2


def tables(length):
    odd = 2 * np.arange(length, dtype=np.int64)[:, None] + 1
    phase = odd * np.arange(length, dtype=np.int64)[None, :] % (4 * length)
    angle = phase.astype(np.float64) * (math.pi / (2 * length))
    return (np.cos(angle), np.sin(angle))


def dot(a, b, dims=((1,), (0,))):
    return lax.dot_general(a, b, (dims, ((), ())), preferred_element_type=F32)


def up(x, axis):
    n = lax.axis_size(axis)
    return lax.ppermute(x, axis, [(i, (i + 1) % n) for i in range(n)])


def down(x, axis):
    n = lax.axis_size(axis)
    return lax.ppermute(x, axis, [(i, (i - 1) % n) for i in range(n)])


def swap(x, axis):
    return lax.ppermute(x, axis, [(0, 1), (1, 0)])


def pick(x, index, axis=0):
    return lax.dynamic_index_in_dim(x, index, axis, keepdims=False)


def ring_gather(block, axis):
    lower = up(block, axis)
    upper = down(block, axis)
    half = block.shape[0] // 2
    far = jnp.concatenate([up(lower[:half], axis), down(upper[half:], axis)], axis=0)
    return [block, upper, far, lower]


def ring_reduce(part, axis):
    far = part(2).astype(BF16)
    half = far.shape[0] // 2
    from_below = up(far[:half], axis).astype(F32)
    from_above = down(far[half:], axis).astype(F32)
    zero = jnp.zeros_like(from_below)
    one = (part(1) + jnp.concatenate([from_below, zero], axis=0)).astype(BF16)
    three = (part(3) + jnp.concatenate([zero, from_above], axis=0)).astype(BF16)
    lower = up(one, axis)
    upper = down(three, axis)
    return part(0) + lower.astype(F32) + upper.astype(F32)


def local(activations, gate_values, in_weight, long_filter, out_cotangent):
    tokens = activations[0]
    gates = gate_values[0].astype(F32)
    upstream = out_cotangent[0].astype(F32)
    groups = X * YL
    replicas = Z * YH * CORE
    block, channels = gates.shape
    features = tokens.shape[1]
    length = block * groups
    part = channels // groups
    rows = in_weight.shape[0]
    taps_rows = block // replicas
    own_rows = rows + taps_rows
    cut = features * 5 // 8
    xi, yi, zi, hi, ci = (lax.axis_index(a) for a in SEQ + REP)
    rep = (zi * YH + hi) * CORE + ci

    cosine, sine = tables(length)
    cos_t = jnp.asarray(cosine.astype(np.float32)).astype(BF16)
    sin_t = jnp.asarray(sine.astype(np.float32)).astype(BF16)

    def spectrum(x):
        return (dot(cos_t, x), dot(sin_t, x))

    def inverse(real, imag):
        return (
            dot(cos_t, real.astype(BF16), ((0,), (0,))) + dot(sin_t, imag.astype(BF16), ((0,), (0,)))
        ) * (1.0 / length)

    early = ring_gather(tokens[:, cut:], "x")
    other = swap(tokens[:, :cut], "yl")
    pair = jnp.where(yi == 0, jnp.concatenate([tokens[:, :cut], other]), jnp.concatenate([other, tokens[:, :cut]]))
    late = ring_gather(pair, "x")
    early_other = swap(jnp.stack(early), "yl")
    acts = jnp.zeros((X, YL, block, features), BF16)
    for k in range(X):
        owner = (xi + k) % X
        acts = lax.dynamic_update_slice(acts, late[k].reshape(1, YL, block, cut), (owner, 0, 0, 0))
        acts = lax.dynamic_update_slice(acts, early[k][None, None], (owner, yi, 0, cut))
        acts = lax.dynamic_update_slice(acts, early_other[k][None, None], (owner, 1 - yi, 0, cut))
    acts = acts.reshape(length, features)

    inner = (upstream * gates).astype(BF16)
    own_taps = lax.dynamic_slice_in_dim(long_filter, rep * taps_rows, taps_rows, 0)
    sent = jnp.concatenate([inner, in_weight, own_taps], axis=0)
    sent = sent.reshape(block + own_rows, groups, part).transpose(1, 0, 2)
    got = lax.all_to_all(sent, SEQ, 0, 0, tiled=True)
    inner = got[:, :block].reshape(length, part)
    piece = got[:, block:]
    other = swap(piece, "yh")
    piece = jnp.where(hi == 0, jnp.stack([piece, other]), jnp.stack([other, piece]))
    ring = ring_gather(piece.reshape(YH * groups, own_rows, part), "z")
    slab = jnp.zeros((Z, YH * groups, own_rows, part), BF16)
    for k in range(Z):
        slab = lax.dynamic_update_slice(slab, ring[k][None], ((zi + k) % Z, 0, 0, 0))
    other = swap(slab, "core")
    slab = jnp.where(ci == 0, jnp.stack([slab, other]), jnp.stack([other, slab]))
    slab = slab.reshape(CORE, Z, YH, groups, own_rows, part).transpose(3, 1, 2, 0, 4, 5)
    weight = slab[..., :rows, :].reshape(features, part)
    taps = slab[..., rows:, :].reshape(length, part)

    f_c, f_s = spectrum(taps)
    i_c, i_s = spectrum(inner)
    value_grad = inverse(f_c * i_c + f_s * i_s, f_c * i_s - f_s * i_c).astype(BF16)

    grad = value_grad.reshape(X, YL, block, part)

    def late_part(k):
        return dot(pick(grad, (xi + k) % X).reshape(YL * block, part), weight[:cut], ((1,), (1,)))

    mine = pick(grad, yi, 1).reshape(X * block, part)
    theirs = pick(grad, 1 - yi, 1).reshape(X * block, part)
    crossed = swap(dot(theirs, weight[cut:], ((1,), (1,))).astype(BF16), "yl")
    late_sum = ring_reduce(late_part, "x").reshape(YL, block, cut)
    late_other = swap(pick(late_sum, 1 - yi).astype(BF16), "yl")
    late_sum = pick(late_sum, yi) + late_other.astype(F32)
    crossed = (dot(mine, weight[cut:], ((1,), (1,))) + crossed.astype(F32)).reshape(X, block, features - cut)
    early_sum = ring_reduce(lambda k: pick(crossed, (xi + k) % X), "x")
    input_grad = jnp.concatenate([late_sum, early_sum], axis=1).astype(BF16)

    values = dot(acts, weight).astype(BF16)
    v_c, v_s = spectrum(values)
    conv = inverse(f_c * v_c - f_s * v_s, f_c * v_s + f_s * v_c)
    conv = lax.all_to_all(conv.astype(BF16).reshape(groups, block, part), SEQ, 0, 0, tiled=True)
    conv = conv.transpose(1, 0, 2).reshape(block, channels).astype(F32)
    mixed_out = (gates * conv).astype(BF16)
    gate_grad = (upstream * conv).astype(BF16)

    scale = 1.0 / math.sqrt(length * replicas)
    filter_part = inverse(v_c * i_c + v_s * i_s, v_c * i_s - v_s * i_c) * scale
    weight_part = dot(acts, value_grad, ((0,), (0,))) * scale
    owned = jnp.concatenate(
        [
            weight_part.reshape(groups, Z, YH, CORE, rows, part),
            filter_part.reshape(groups, Z, YH, CORE, taps_rows, part),
        ],
        axis=4,
    )
    other = swap(pick(owned, 1 - ci, 3).astype(BF16), "core")
    owned = pick(owned, ci, 3) + other.astype(F32)
    owned = ring_reduce(lambda k: pick(owned, (zi + k) % Z, 1), "z")
    owned = lax.all_to_all(owned.reshape(groups * YH, own_rows, part), SEQ + ("yh",), 0, 0, tiled=True)
    owned = jnp.sum(owned.reshape(groups, YH, own_rows, part), axis=1)
    owned = owned.transpose(1, 0, 2).reshape(own_rows, channels)
    return (mixed_out[None], gate_grad[None], input_grad[None], owned[:rows], owned[rows:])


def solution(mesh):
    mesh = Mesh(mesh.devices.reshape(X, YL, Z, YH, CORE), SEQ + REP)
    split = P(REP, SEQ, None)
    in_specs = (split, split, P(SEQ + REP, None), P(SEQ, None), split)
    out_specs = (split, split, split, P(SEQ + REP, None), P(SEQ + REP, None))
    return jax.shard_map(local, mesh=mesh, in_specs=in_specs, out_specs=out_specs, check_vma=False)
```

```python
import math

import jax
import jax.numpy as jnp
import numpy as np
from jax import lax
from jax.experimental import pallas as pl
from jax.experimental.pallas import tpu as pltpu
from jax.sharding import Mesh
from jax.sharding import PartitionSpec as P

F32 = jnp.float32
BF16 = jnp.bfloat16
SEQ = ("x", "yl")
REP = ("z", "yh", "core")
X, YL, Z, YH, CORE = 4, 2, 4, 2, 2
ROWS = 256


def tables(length):
    odd = 2 * np.arange(length, dtype=np.int64)[:, None] + 1
    phase = odd * np.arange(length, dtype=np.int64)[None, :] % (4 * length)
    angle = phase.astype(np.float64) * (math.pi / (2 * length))
    return (np.cos(angle), np.sin(angle))


def dot(a, b):
    return jnp.dot(a, b, preferred_element_type=F32)


def up(x, axis):
    n = lax.axis_size(axis)
    return lax.ppermute(x, axis, [(i, (i + 1) % n) for i in range(n)])


def down(x, axis):
    n = lax.axis_size(axis)
    return lax.ppermute(x, axis, [(i, (i - 1) % n) for i in range(n)])


def swap(x, axis):
    return lax.ppermute(x, axis, [(0, 1), (1, 0)])


def pick(x, index, axis=0):
    return lax.dynamic_index_in_dim(x, index, axis, keepdims=False)


def halves_round(block, axis):
    lower = up(block, axis)
    upper = down(block, axis)
    half = block.shape[0] // 2
    return block, upper, lower, up(lower[:half], axis), down(upper[half:], axis)


def in_order(own, other, index):
    return jnp.where(index == 0, jnp.stack([own, other]), jnp.stack([other, own]))


def ring_gather(block, axis):
    own, upper, lower, far_a, far_b = halves_round(block, axis)
    me = lax.axis_index(axis)
    out = jnp.zeros((4,) + block.shape, block.dtype)
    for k, piece in ((0, own), (1, upper), (3, lower), (2, jnp.concatenate([far_a, far_b]))):
        out = lax.dynamic_update_index_in_dim(out, piece, (me + k) % 4, 0)
    return out


def transforms_body(
    core, got, weight, taps, cos, sin, cos_t, sin_t, pair_o, w_mine, w_send, f_mine, f_send,
    acts_v, inner_v, w_v, taps_v, c_v, s_v, ct_v, st_v, fc, fs, ic, js, vc, vs, p, q, vals, sem,
):
    groups, block, features = acts_v.shape
    length, part = vals.shape
    scale = 1.0 / math.sqrt(length * Z * YH * CORE)
    moves = (
        (taps, taps_v),
        (cos, c_v),
        (sin, s_v),
        (got.at[:, :, features:], inner_v),
        (cos_t, ct_v),
        (sin_t, st_v),
        (weight, w_v),
        (got.at[:, :, :features], acts_v),
    )
    copies = [pltpu.make_async_copy(a, b, sem.at[i]) for i, (a, b) in enumerate(moves)]
    for copy in copies:
        copy.start()
    acts = acts_v.reshape(length, features)
    inner = inner_v.reshape(length, part)
    per = ROWS // block

    def each(count, step):
        @pl.loop(0, count // ROWS)
        def _(i):
            step(i, pl.ds(pl.multiple_of(i * ROWS, ROWS), ROWS))

    def spectrum(x, cos_sum, sin_sum):
        def step(i, r):
            cos_sum[r, :] = dot(c_v[r, :], x[...])
            sin_sum[r, :] = dot(s_v[r, :], x[...])

        each(length, step)

    def product(fn):
        def step(i, r):
            a, b = fn(r)
            p[r, :] = a.astype(BF16)
            q[r, :] = b.astype(BF16)

        each(length, step)

    def inverse(r):
        return (dot(ct_v[r, :], p[...]) + dot(st_v[r, :], q[...])) * (1.0 / length)

    def by_core(x, rows):
        x = x.reshape(-1, CORE, rows, part)
        own = core[0] == 0
        return jnp.where(own, x[:, 0], x[:, 1]), jnp.where(own, x[:, 1], x[:, 0])

    for copy in copies[:3]:
        copy.wait()
    spectrum(taps_v, fc, fs)
    copies[3].wait()
    spectrum(inner, ic, js)
    product(lambda r: (fc[r, :] * ic[r, :] + fs[r, :] * js[r, :], fc[r, :] * js[r, :] - fs[r, :] * ic[r, :]))
    copies[4].wait()
    copies[5].wait()

    def grad_step(i, r):
        g = inverse(r).astype(BF16)
        vals[r, :] = g
        pair_o[pl.ds(i * per, per), :, part:] = g.reshape(per, block, part)

    each(length, grad_step)
    copies[6].wait()
    copies[7].wait()

    def weight_step(i, r):
        g = lax.dot_general(acts[:, r], vals[...], (((0,), (0,)), ((), ())), preferred_element_type=F32) * scale
        own, other = by_core(g, 16)
        n = ROWS // (CORE * 16)
        w_mine[pl.ds(i * n, n)] = own
        w_send[pl.ds(i * n, n)] = other.astype(BF16)

    each(features, weight_step)

    def value_step(i, r):
        vals[r, :] = dot(acts[r, :], w_v[...]).astype(BF16)

    each(length, value_step)
    spectrum(vals, vc, vs)
    product(lambda r: (fc[r, :] * vc[r, :] - fs[r, :] * vs[r, :], fc[r, :] * vs[r, :] + fs[r, :] * vc[r, :]))

    def conv_step(i, r):
        pair_o[pl.ds(i * per, per), :, :part] = inverse(r).astype(BF16).reshape(per, block, part)

    each(length, conv_step)
    product(lambda r: (vc[r, :] * ic[r, :] + vs[r, :] * js[r, :], vc[r, :] * js[r, :] - vs[r, :] * ic[r, :]))

    def filter_step(i, r):
        own, other = by_core(inverse(r) * scale, 8)
        n = ROWS // (CORE * 8)
        f_mine[pl.ds(i * n, n)] = own
        f_send[pl.ds(i * n, n)] = other

    each(length, filter_step)


def transforms(core, got, weight, taps, tables_v):
    groups, block, width = got.shape
    features, part = weight.shape
    length = groups * block
    away = pl.BlockSpec(memory_space=pl.ANY)
    near = pl.BlockSpec(memory_space=pltpu.VMEM)
    shape = jax.ShapeDtypeStruct
    own = features // (CORE * 16)
    wave = pltpu.VMEM((length, part), F32)
    narrow = pltpu.VMEM((length, part), BF16)
    table = pltpu.VMEM((length, length), BF16)
    return pl.pallas_call(
        transforms_body,
        out_shape=[
            shape((groups, block, 2 * part), BF16),
            shape((own, 16, part), F32),
            shape((own, 16, part), BF16),
            shape((own, 8, part), F32),
            shape((own, 8, part), F32),
        ],
        in_specs=[pl.BlockSpec(memory_space=pltpu.SMEM)] + [away] * 7,
        out_specs=[near] * 5,
        scratch_shapes=[
            pltpu.VMEM((groups, block, features), BF16),
            pltpu.VMEM((groups, block, part), BF16),
            pltpu.VMEM((features, part), BF16),
            narrow,
            table,
            table,
            table,
            table,
            wave,
            wave,
            wave,
            wave,
            wave,
            wave,
            narrow,
            narrow,
            narrow,
            pltpu.SemaphoreType.DMA((8,)),
        ],
        compiler_params=pltpu.CompilerParams(vmem_limit_bytes=48 * 2**20),
        name="transforms",
    )(core, got, weight, taps, *tables_v)


def outputs_body(place, back, gates, upstream, *refs):
    pieces, (mixed_o, gate_o, input_o, w_v, grad_v, sem) = refs[:10], refs[10:]
    groups, block, _ = back.shape
    part = back.shape[2] // 2
    z, core = place[0], place[1]
    copies = []
    for side, which in ((0, core), (1, 1 - core)):
        own, upper, lower, far_a, far_b = pieces[5 * side : 5 * side + 5]
        for k, ref, yh in ((0, own, None), (1, upper, None), (3, lower, None), (2, far_a, 0), (2, far_b, 1)):
            to = lax.rem(z + k, Z)
            for h in (0, 1) if yh is None else (yh,):
                src = ref.at[h if yh is None else 0]
                copies.append(pltpu.make_async_copy(src, w_v.at[:, to, h, which], sem.at[len(copies)]))
    for copy in copies:
        copy.start()
    for g in range(groups):
        c = pl.ds(g * part, part)
        conv = back[g, :, :part].astype(F32)
        mixed_o[:, c] = (gates[:, c].astype(F32) * conv).astype(BF16)
        gate_o[:, c] = (upstream[:, c].astype(F32) * conv).astype(BF16)
        grad_v[:, c] = back[g, :, part:]
    for copy in copies:
        copy.wait()
    rows = w_v.shape[4]
    for g in range(groups):
        w = w_v[g].reshape(Z * YH * CORE * rows, w_v.shape[5])
        n = w.shape[0]
        y = lax.dot_general(grad_v[...], w, (((1,), (1,)), ((), ())), preferred_element_type=F32)
        input_o[:, pl.ds(g * n, n)] = y.astype(BF16)


def outputs(place, back, gates, upstream, pieces):
    groups, block, _ = back.shape
    channels = gates.shape[1]
    rows = pieces[0].shape[2]
    features = groups * Z * YH * CORE * rows
    away = pl.BlockSpec(memory_space=pl.ANY)
    near = pl.BlockSpec(memory_space=pltpu.VMEM)
    shape = jax.ShapeDtypeStruct
    return pl.pallas_call(
        outputs_body,
        out_shape=[shape((block, channels), BF16)] * 2 + [shape((block, features), BF16)],
        in_specs=[pl.BlockSpec(memory_space=pltpu.SMEM)] + [near] * 3 + [away] * 10,
        out_specs=[near] * 3,
        scratch_shapes=[
            pltpu.VMEM((groups, Z, YH, CORE, rows, channels), BF16),
            pltpu.VMEM((block, channels), BF16),
            pltpu.SemaphoreType.DMA((16,)),
        ],
        compiler_params=pltpu.CompilerParams(vmem_limit_bytes=32 * 2**20),
        name="outputs",
    )(place, back, gates, upstream, *pieces)


def local(activations, gate_values, in_weight, long_filter, out_cotangent):
    tokens = activations[0]
    gates = gate_values[0]
    upstream = out_cotangent[0]
    groups = X * YL
    replicas = Z * YH * CORE
    block, channels = gates.shape
    features = tokens.shape[1]
    length = block * groups
    part = channels // groups
    rows = in_weight.shape[0]
    taps_rows = block // replicas
    own_rows = rows + taps_rows
    xi, yi, zi, hi, ci = (lax.axis_index(a) for a in SEQ + REP)

    cosine, sine = (jnp.asarray(t.astype(np.float32)).astype(BF16) for t in tables(length))
    cosine_t, sine_t = (jnp.asarray(t.T.astype(np.float32)).astype(BF16) for t in tables(length))

    inner = (upstream.astype(F32) * gates.astype(F32)).astype(BF16)
    inner = inner.reshape(block, groups, part).transpose(1, 0, 2)
    sent = jnp.concatenate([jnp.broadcast_to(tokens, (groups, block, features)), inner], axis=2)
    got = lax.all_to_all(sent, SEQ, 0, 0, tiled=True)

    own_taps = lax.dynamic_slice_in_dim(long_filter, ((zi * YH + hi) * CORE + ci) * taps_rows, taps_rows, 0)
    piece = jnp.concatenate([in_weight, own_taps], axis=0)
    piece = ring_gather(in_order(piece, swap(piece, "yl"), yi), "x").reshape(groups, own_rows, channels)
    thin = lax.dynamic_slice_in_dim(piece, (xi * YL + yi) * part, part, 2)
    thin = ring_gather(in_order(thin, swap(thin, "yh"), hi), "z")
    thin = in_order(thin, swap(thin, "core"), ci).transpose(3, 1, 2, 0, 4, 5)
    weight = thin[..., :rows, :].reshape(features, part)
    taps = thin[..., rows:, :].reshape(length, part)
    wide = piece[:, :rows]
    wide = halves_round(in_order(wide, swap(wide, "yh"), hi), "z")
    wide = wide + tuple(swap(w, "core") for w in wide)

    pair, w_mine, w_send, f_mine, f_send = transforms(
        ci.reshape(1), got, weight, taps, (cosine, sine, cosine_t, sine_t)
    )

    back = lax.all_to_all(pair, SEQ, 0, 0, tiled=True)
    other = swap(jnp.concatenate([w_send, f_send.astype(BF16)], axis=1), "core")
    owned = (jnp.concatenate([w_mine, f_mine], axis=1) + other.astype(F32)).astype(BF16)
    owned = lax.all_to_all(owned, SEQ + ("z", "yh"), 0, 0, tiled=True)
    owned = jnp.sum(owned.reshape(groups, Z * YH, own_rows, part).astype(F32), axis=1)
    owned = owned.transpose(1, 0, 2).reshape(own_rows, channels)

    mixed_out, gate_grad, input_grad = outputs(jnp.stack([zi, ci]), back, gates, upstream, wide)
    return (mixed_out[None], gate_grad[None], input_grad[None], owned[:rows], owned[rows:])


def solution(mesh):
    mesh = Mesh(mesh.devices.reshape(X, YL, Z, YH, CORE), SEQ + REP)
    split = P(REP, SEQ, None)
    in_specs = (split, split, P(SEQ + REP, None), P(SEQ, None), split)
    out_specs = (split, split, split, P(SEQ + REP, None), P(SEQ + REP, None))
    return jax.shard_map(local, mesh=mesh, in_specs=in_specs, out_specs=out_specs, check_vma=False)
```

```python
import math

import jax
import jax.numpy as jnp
import numpy as np
from jax import lax
from jax.experimental import pallas as pl
from jax.experimental.pallas import tpu as pltpu
from jax.sharding import Mesh
from jax.sharding import PartitionSpec as P

F32 = jnp.float32
BF16 = jnp.bfloat16
SEQ = ("x", "yl")
REP = ("z", "yh", "core")
X, YL, Z, YH, CORE = 4, 2, 4, 2, 2
ROWS = 256


def tables(length):
    odd = 2 * np.arange(length, dtype=np.int64)[:, None] + 1
    phase = odd * np.arange(length, dtype=np.int64)[None, :] % (4 * length)
    angle = phase.astype(np.float64) * (math.pi / (2 * length))
    return (np.cos(angle), np.sin(angle))


def dot(a, b):
    return jnp.dot(a, b, preferred_element_type=F32)


def up(x, axis):
    n = lax.axis_size(axis)
    return lax.ppermute(x, axis, [(i, (i + 1) % n) for i in range(n)])


def down(x, axis):
    n = lax.axis_size(axis)
    return lax.ppermute(x, axis, [(i, (i - 1) % n) for i in range(n)])


def swap(x, axis):
    return lax.ppermute(x, axis, [(0, 1), (1, 0)])


def pick(x, index, axis=0):
    return lax.dynamic_index_in_dim(x, index, axis, keepdims=False)


def halves_round(block, axis):
    lower = up(block, axis)
    upper = down(block, axis)
    half = block.shape[0] // 2
    return block, upper, lower, up(lower[:half], axis), down(upper[half:], axis)


def in_order(own, other, index):
    return jnp.where(index == 0, jnp.stack([own, other]), jnp.stack([other, own]))


def places(position, size):
    far = lax.rem(position + 2, size)
    return (
        (position, None),
        (lax.rem(position + 1, size), None),
        (lax.rem(position + size - 1, size), None),
        (far, 0),
        (far, 1),
    )


def transforms_body(place, *refs):
    slices, (cos, sin, cos_t, sin_t), thin, late, early, early_own, early_far, rest = (
        refs[0], refs[1:5], refs[5:10], refs[10:15], refs[15:20], refs[20], refs[21], refs[22:]
    )
    (
        pair_o, mine_o, send_o, acts_v, inner_v, w_v, taps_v, c_v, s_v, ct_v, st_v, fc, fs, ic, js, vc, vs, p, q,
        vals, sem,
    ) = rest
    xs, yls, block, features = acts_v.shape
    groups = xs * yls
    length, part = vals.shape
    scale = 1.0 / math.sqrt(length * Z * YH * CORE)
    x, yl, z, core = (place[i] for i in range(4))
    cut = late[0].shape[2]
    half = taps_v.shape[4] // CORE
    copies = []

    def move(src, dst):
        copies.append(pltpu.make_async_copy(src, dst, sem.at[len(copies)]))
        copies[-1].start()

    def waiter(first, last):
        def wait():
            for copy in copies[first:last]:
                copy.wait()

        return wait

    for ref, (to, side) in zip(thin, places(z, Z)):
        for n in (0, 1) if side is None else (side,):
            c = core if n == 0 else 1 - core
            src = ref.at[n if side is None else 0]
            move(src.at[:, :, :, part:], taps_v.at[:, to, :, :, pl.ds(pl.multiple_of(c * half, half), half)])
    move(cos, c_v)
    move(sin, s_v)
    wait_taps = waiter(0, len(copies))
    mark = len(copies)
    lines = slices.shape[1]
    for n in range(block // lines):
        left = slices.shape[2] - part * (block // lines - n)
        move(slices.at[:, :, left : left + part], inner_v.at[:, n * lines : (n + 1) * lines, :])
    wait_inner = waiter(mark, len(copies))
    mark = len(copies)
    move(cos_t, ct_v)
    move(sin_t, st_v)
    wait_inverse = waiter(mark, len(copies))
    mark = len(copies)
    for ref, (to, side) in zip(late, places(x, X)):
        if side is None:
            move(ref, acts_v.at[to, :, :, :cut])
        else:
            move(ref.at[0], acts_v.at[to, side, :, :cut])
    n = block // 2
    for i, (ref, (to, side)) in enumerate(zip(early, places(x, X))):
        across = early_own.at[i] if side is None else early_far.at[side]
        for src, y in ((ref, yl), (across, 1 - yl)):
            dst = acts_v.at[to, y]
            if side is None:
                move(src, dst.at[:, cut:])
            else:
                move(src, dst.at[side * n : (side + 1) * n, cut:])
    wait_acts = waiter(mark, len(copies))
    mark = len(copies)
    for ref, (to, side) in zip(thin, places(z, Z)):
        for n in (0, 1) if side is None else (side,):
            c = core if n == 0 else 1 - core
            src = ref.at[n if side is None else 0]
            move(src.at[:, :, :, :part], w_v.at[:, to, :, c])
    wait_weight = waiter(mark, len(copies))
    weight = w_v.reshape(features, part)
    taps = taps_v.reshape(length, part)
    acts = acts_v.reshape(length, features)
    inner = inner_v.reshape(length, part)
    per = ROWS // block

    def each(count, step):
        @pl.loop(0, count // ROWS)
        def _(i):
            step(i, pl.ds(pl.multiple_of(i * ROWS, ROWS), ROWS))

    def spectrum(x, cos_sum, sin_sum):
        def step(i, r):
            cos_sum[r, :] = dot(c_v[r, :], x[...])
            sin_sum[r, :] = dot(s_v[r, :], x[...])

        each(length, step)

    def product(fn):
        def step(i, r):
            a, b = fn(r)
            p[r, :] = a.astype(BF16)
            q[r, :] = b.astype(BF16)

        each(length, step)

    def inverse(r):
        return (dot(ct_v[r, :], p[...]) + dot(st_v[r, :], q[...])) * (1.0 / length)

    def by_core(x, rows):
        x = x.reshape(-1, CORE, rows, part)
        own = core == 0
        return jnp.where(own, x[:, 0], x[:, 1]), jnp.where(own, x[:, 1], x[:, 0])

    wait_taps()
    spectrum(taps, fc, fs)
    wait_inner()
    spectrum(inner, ic, js)
    product(lambda r: (fc[r, :] * ic[r, :] + fs[r, :] * js[r, :], fc[r, :] * js[r, :] - fs[r, :] * ic[r, :]))
    wait_inverse()

    def grad_step(i, r):
        g = inverse(r).astype(BF16)
        vals[r, :] = g
        pair_o[pl.ds(i * per, per), :, part:] = g.reshape(per, block, part)

    each(length, grad_step)
    wait_acts()

    def weight_step(i, r):
        g = lax.dot_general(acts[:, r], vals[...], (((0,), (0,)), ((), ())), preferred_element_type=F32) * scale
        own, other = by_core(g, 16)
        n = ROWS // (CORE * 16)
        mine_o[pl.ds(i * n, n), :16] = own
        send_o[pl.ds(i * n, n), :16] = other

    each(features, weight_step)
    wait_weight()

    def value_step(i, r):
        vals[r, :] = dot(acts[r, :], weight[...]).astype(BF16)

    each(length, value_step)
    spectrum(vals, vc, vs)
    product(lambda r: (fc[r, :] * vc[r, :] - fs[r, :] * vs[r, :], fc[r, :] * vs[r, :] + fs[r, :] * vc[r, :]))

    def conv_step(i, r):
        pair_o[pl.ds(i * per, per), :, :part] = inverse(r).astype(BF16).reshape(per, block, part)

    each(length, conv_step)
    product(lambda r: (vc[r, :] * ic[r, :] + vs[r, :] * js[r, :], vc[r, :] * js[r, :] - vs[r, :] * ic[r, :]))

    def filter_step(i, r):
        own, other = by_core(inverse(r) * scale, 8)
        n = ROWS // (CORE * 8)
        mine_o[pl.ds(i * n, n), 16:] = own
        send_o[pl.ds(i * n, n), 16:] = other

    each(length, filter_step)


def transforms(place, slices, tables_v, thin, late, early, early_own, early_far):
    length = tables_v[0].shape[0]
    block = length // (X * YL)
    part = thin[0].shape[4] * 2 // 3
    features = late[0].shape[2] + early[0].shape[1]
    away = pl.BlockSpec(memory_space=pl.ANY)
    near = pl.BlockSpec(memory_space=pltpu.VMEM)
    shape = jax.ShapeDtypeStruct
    own = features // (CORE * 16)
    wave = pltpu.VMEM((length, part), F32)
    narrow = pltpu.VMEM((length, part), BF16)
    table = pltpu.VMEM((length, length), BF16)
    operands = (slices, *tables_v, *thin, *late, *early, early_own, early_far)
    return pl.pallas_call(
        transforms_body,
        out_shape=[shape((X * YL, block, 2 * part), BF16)] + [shape((own, 24, part), F32)] * 2,
        in_specs=[pl.BlockSpec(memory_space=pltpu.SMEM)] + [away] * len(operands),
        out_specs=[near] * 3,
        scratch_shapes=[
            pltpu.VMEM((X, YL, block, features), BF16),
            pltpu.VMEM((X * YL, block, part), BF16),
            pltpu.VMEM((X * YL, Z, YH, CORE, 16, part), BF16),
            pltpu.VMEM((X * YL, Z, YH, 16, part), BF16),
            *[table] * 4,
            *[wave] * 6,
            *[narrow] * 3,
            pltpu.SemaphoreType.DMA((48,)),
        ],
        compiler_params=pltpu.CompilerParams(vmem_limit_bytes=48 * 2**20),
        name="transforms",
    )(place, *operands)


def outputs_body(place, back, gates, upstream, *refs):
    pieces, (mixed_o, gate_o, input_o, w_v, grad_v, sem) = refs[:10], refs[10:]
    groups, block, _ = back.shape
    part = back.shape[2] // 2
    z, core = place[2], place[3]
    copies = []
    for n, c in ((0, core), (1, 1 - core)):
        for ref, (to, side) in zip(pieces[5 * n : 5 * n + 5], places(z, Z)):
            some = pl.ds(0, groups) if side is None else pl.ds(side * groups // 2, groups // 2)
            copies.append(pltpu.make_async_copy(ref, w_v.at[some, to, :, c], sem.at[len(copies)]))
    for copy in copies:
        copy.start()
    for g in range(groups):
        c = pl.ds(g * part, part)
        conv = back[g, :, :part].astype(F32)
        mixed_o[:, c] = (gates[:, c].astype(F32) * conv).astype(BF16)
        gate_o[:, c] = (upstream[:, c].astype(F32) * conv).astype(BF16)
        grad_v[:, c] = back[g, :, part:]
    for copy in copies:
        copy.wait()
    rows = w_v.shape[4]
    for g in range(groups):
        w = w_v[g].reshape(Z * YH * CORE * rows, w_v.shape[5])
        n = w.shape[0]
        y = lax.dot_general(grad_v[...], w, (((1,), (1,)), ((), ())), preferred_element_type=F32)
        input_o[:, pl.ds(g * n, n)] = y.astype(BF16)


def outputs(place, back, gates, upstream, pieces):
    groups, block, _ = back.shape
    channels = gates.shape[1]
    rows = pieces[0].shape[2]
    features = groups * Z * YH * CORE * rows
    away = pl.BlockSpec(memory_space=pl.ANY)
    near = pl.BlockSpec(memory_space=pltpu.VMEM)
    shape = jax.ShapeDtypeStruct
    return pl.pallas_call(
        outputs_body,
        out_shape=[shape((block, channels), BF16)] * 2 + [shape((block, features), BF16)],
        in_specs=[pl.BlockSpec(memory_space=pltpu.SMEM)] + [near] * 3 + [away] * 10,
        out_specs=[near] * 3,
        scratch_shapes=[
            pltpu.VMEM((groups, Z, YH, CORE, rows, channels), BF16),
            pltpu.VMEM((block, channels), BF16),
            pltpu.SemaphoreType.DMA((10,)),
        ],
        compiler_params=pltpu.CompilerParams(vmem_limit_bytes=32 * 2**20),
        name="outputs",
    )(place, back, gates, upstream, *pieces)


def local(activations, gate_values, in_weight, long_filter, out_cotangent):
    tokens = activations[0]
    gates = gate_values[0]
    upstream = out_cotangent[0]
    groups = X * YL
    replicas = Z * YH * CORE
    block, channels = gates.shape
    features = tokens.shape[1]
    length = block * groups
    part = channels // groups
    rows = in_weight.shape[0]
    shared = rows
    half = part // CORE
    cut = features * 5 // 8
    xi, yi, zi, hi, ci = (lax.axis_index(a) for a in SEQ + REP)
    place = jnp.stack([xi, yi, zi, ci])

    cosine, sine = (jnp.asarray(t.astype(np.float32)).astype(BF16) for t in tables(length))
    cosine_t, sine_t = (jnp.asarray(t.T.astype(np.float32)).astype(BF16) for t in tables(length))

    own_taps = lax.dynamic_slice_in_dim(long_filter, (zi * YH + hi) * shared, shared, 0)
    own_taps = pick(own_taps.reshape(shared, groups, CORE, half), ci, 2).reshape(shared, groups * half)
    piece = jnp.concatenate([in_weight, own_taps], axis=1)
    piece = in_order(piece, swap(piece, "yh"), hi).reshape(YH * rows, channels + groups * half)
    inner = (upstream.astype(F32) * gates.astype(F32)).astype(BF16)
    inner = inner.reshape(block // (YH * rows), YH * rows, groups, part).transpose(2, 1, 0, 3)
    sent = jnp.concatenate(
        [
            jnp.broadcast_to(piece[:, :channels], (groups, YH * rows, channels)),
            piece[:, channels:].reshape(YH * rows, groups, half).transpose(1, 0, 2),
            inner.reshape(groups, YH * rows, -1),
        ],
        axis=2,
    )
    slices = lax.all_to_all(sent, SEQ, 0, 0, tiled=True)

    thin = jnp.concatenate(
        [
            lax.dynamic_slice_in_dim(slices, (xi * YL + yi) * part, part, 2),
            slices[:, :, channels : channels + half],
        ],
        axis=2,
    ).reshape(groups, YH, rows, part + half)
    thin = halves_round(jnp.stack([thin, swap(thin, "core")]), "z")
    wide = halves_round(slices[:, :, :channels].reshape(groups, YH, rows, channels), "z")
    wide = wide + tuple(swap(w, "core") for w in wide)

    early = halves_round(tokens[:, cut:], "x")
    late = halves_round(in_order(tokens[:, :cut], swap(tokens[:, :cut], "yl"), yi), "x")
    early_own = swap(jnp.stack(early[:3]), "yl")
    early_far = swap(jnp.stack(early[3:]), "yl")

    pair, mine, other = transforms(
        place, slices, (cosine, sine, cosine_t, sine_t), thin, late, early, early_own, early_far
    )

    back = lax.all_to_all(pair, SEQ, 0, 0, tiled=True)
    owned = (mine + swap(other, "core")).astype(BF16)
    owned = lax.all_to_all(owned, SEQ + ("z", "yh"), 0, 0, tiled=True)
    owned = jnp.sum(owned.reshape(groups, Z * YH, -1, part).astype(F32), axis=1)
    owned = owned.transpose(1, 0, 2).reshape(-1, channels)

    mixed_out, gate_grad, input_grad = outputs(place, back, gates, upstream, wide)
    return (mixed_out[None], gate_grad[None], input_grad[None], owned[:rows], owned[rows:])


def solution(mesh):
    mesh = Mesh(mesh.devices.reshape(X, YL, Z, YH, CORE), SEQ + REP)
    split = P(REP, SEQ, None)
    in_specs = (split, split, P(SEQ + REP, None), P(SEQ, None), split)
    out_specs = (split, split, split, P(SEQ + REP, None), P(SEQ + REP, None))
    return jax.shard_map(local, mesh=mesh, in_specs=in_specs, out_specs=out_specs, check_vma=False)
```

```python
import math

import jax
import jax.numpy as jnp
import numpy as np
from jax import lax
from jax.experimental import pallas as pl
from jax.experimental.pallas import tpu as pltpu
from jax.sharding import Mesh
from jax.sharding import PartitionSpec as P

F32 = jnp.float32
BF16 = jnp.bfloat16
SEQ = ("x", "yl")
REP = ("z", "yh", "core")
X, YL, Z, YH, CORE = 4, 2, 4, 2, 2
ROWS = 256
WIDE = ((0, None), (1, 0), (1, 1), (3, 0), (3, 1), (2, 0), (2, 1))


def tables(length):
    odd = 2 * np.arange(length, dtype=np.int64)[:, None] + 1
    phase = odd * np.arange(length, dtype=np.int64)[None, :] % (4 * length)
    angle = phase.astype(np.float64) * (math.pi / (2 * length))
    return (np.cos(angle), np.sin(angle))


def dot(a, b):
    return jnp.dot(a, b, preferred_element_type=F32)


def up(x, axis):
    n = lax.axis_size(axis)
    return lax.ppermute(x, axis, [(i, (i + 1) % n) for i in range(n)])


def down(x, axis):
    n = lax.axis_size(axis)
    return lax.ppermute(x, axis, [(i, (i - 1) % n) for i in range(n)])


def swap(x, axis):
    return lax.ppermute(x, axis, [(0, 1), (1, 0)])


def pick(x, index, axis=0):
    return lax.dynamic_index_in_dim(x, index, axis, keepdims=False)


def halves_round(block, axis):
    lower = up(block, axis)
    upper = down(block, axis)
    half = block.shape[0] // 2
    return block, upper, lower, up(lower[:half], axis), down(upper[half:], axis)


def after(x, *others):
    return lax.optimization_barrier((x, *others))[0]


def in_order(own, other, index):
    return jnp.where(index == 0, jnp.stack([own, other]), jnp.stack([other, own]))


def places(position, size):
    far = lax.rem(position + 2, size)
    return (
        (position, None),
        (lax.rem(position + 1, size), None),
        (lax.rem(position + size - 1, size), None),
        (far, 0),
        (far, 1),
    )


def transforms_body(place, *refs):
    slices, (cos, sin, cos_t, sin_t), thin, late, early, early_own, early_far, rest = (
        refs[0], refs[1:5], refs[5:10], refs[10:15], refs[15:20], refs[20], refs[21], refs[22:]
    )
    (
        pair_o, mine_o, send_o, acts_v, inner_v, w_v, taps_v, c_v, s_v, ct_v, st_v, fc, fs, ic, js, vc, vs, p, q,
        vals, sem,
    ) = rest
    xs, yls, block, features = acts_v.shape
    groups = xs * yls
    length, part = vals.shape
    scale = 1.0 / math.sqrt(length * Z * YH * CORE)
    x, yl, z, core = (place[i] for i in range(4))
    cut = late[0].shape[2]
    half = taps_v.shape[4] // CORE
    copies = []

    def move(src, dst):
        copies.append(pltpu.make_async_copy(src, dst, sem.at[len(copies)]))
        copies[-1].start()

    def waiter(first, last):
        def wait():
            for copy in copies[first:last]:
                copy.wait()

        return wait

    for ref, (to, side) in zip(thin, places(z, Z)):
        for n in (0, 1) if side is None else (side,):
            c = core if n == 0 else 1 - core
            src = ref.at[n if side is None else 0]
            move(src.at[:, :, :, part:], taps_v.at[:, to, :, :, pl.ds(pl.multiple_of(c * half, half), half)])
    move(cos, c_v)
    move(sin, s_v)
    wait_taps = waiter(0, len(copies))
    mark = len(copies)
    lines = slices.shape[1]
    for n in range(block // lines):
        left = slices.shape[2] - part * (block // lines - n)
        move(slices.at[:, :, left : left + part], inner_v.at[:, n * lines : (n + 1) * lines, :])
    wait_inner = waiter(mark, len(copies))
    mark = len(copies)
    move(cos_t, ct_v)
    move(sin_t, st_v)
    wait_inverse = waiter(mark, len(copies))
    mark = len(copies)
    for ref, (to, side) in zip(late, places(x, X)):
        if side is None:
            move(ref, acts_v.at[to, :, :, :cut])
        else:
            move(ref.at[0], acts_v.at[to, side, :, :cut])
    n = block // 2
    for i, (ref, (to, side)) in enumerate(zip(early, places(x, X))):
        across = early_own.at[i] if side is None else early_far.at[side]
        for src, y in ((ref, yl), (across, 1 - yl)):
            dst = acts_v.at[to, y]
            if side is None:
                move(src, dst.at[:, cut:])
            else:
                move(src, dst.at[side * n : (side + 1) * n, cut:])
    wait_acts = waiter(mark, len(copies))
    mark = len(copies)
    for ref, (to, side) in zip(thin, places(z, Z)):
        for n in (0, 1) if side is None else (side,):
            c = core if n == 0 else 1 - core
            src = ref.at[n if side is None else 0]
            move(src.at[:, :, :, :part], w_v.at[:, to, :, c])
    wait_weight = waiter(mark, len(copies))
    weight = w_v.reshape(features, part)
    taps = taps_v.reshape(length, part)
    acts = acts_v.reshape(length, features)
    inner = inner_v.reshape(length, part)
    per = ROWS // block

    def each(count, step):
        @pl.loop(0, count // ROWS)
        def _(i):
            step(i, pl.ds(pl.multiple_of(i * ROWS, ROWS), ROWS))

    def spectrum(x, cos_sum, sin_sum):
        def step(i, r):
            cos_sum[r, :] = dot(c_v[r, :], x[...])
            sin_sum[r, :] = dot(s_v[r, :], x[...])

        each(length, step)

    def product(fn):
        def step(i, r):
            a, b = fn(r)
            p[r, :] = a.astype(BF16)
            q[r, :] = b.astype(BF16)

        each(length, step)

    def inverse(r):
        return (dot(ct_v[r, :], p[...]) + dot(st_v[r, :], q[...])) * (1.0 / length)

    def by_core(x, rows):
        x = x.reshape(-1, CORE, rows, part)
        own = core == 0
        return jnp.where(own, x[:, 0], x[:, 1]), jnp.where(own, x[:, 1], x[:, 0])

    wait_taps()
    spectrum(taps, fc, fs)
    wait_inner()
    spectrum(inner, ic, js)
    product(lambda r: (fc[r, :] * ic[r, :] + fs[r, :] * js[r, :], fc[r, :] * js[r, :] - fs[r, :] * ic[r, :]))
    wait_inverse()

    def grad_step(i, r):
        g = inverse(r).astype(BF16)
        vals[r, :] = g
        pair_o[pl.ds(i * per, per), :, part:] = g.reshape(per, block, part)

    each(length, grad_step)
    wait_acts()

    def weight_step(i, r):
        g = lax.dot_general(acts[:, r], vals[...], (((0,), (0,)), ((), ())), preferred_element_type=F32) * scale
        own, other = by_core(g, 16)
        n = ROWS // (CORE * 16)
        mine_o[pl.ds(i * n, n), :16] = own
        send_o[pl.ds(i * n, n), :16] = other

    each(features, weight_step)
    wait_weight()

    def value_step(i, r):
        vals[r, :] = dot(acts[r, :], weight[...]).astype(BF16)

    each(length, value_step)
    spectrum(vals, vc, vs)
    product(lambda r: (fc[r, :] * vc[r, :] - fs[r, :] * vs[r, :], fc[r, :] * vs[r, :] + fs[r, :] * vc[r, :]))

    def conv_step(i, r):
        pair_o[pl.ds(i * per, per), :, :part] = inverse(r).astype(BF16).reshape(per, block, part)

    each(length, conv_step)
    product(lambda r: (vc[r, :] * ic[r, :] + vs[r, :] * js[r, :], vc[r, :] * js[r, :] - vs[r, :] * ic[r, :]))

    def filter_step(i, r):
        own, other = by_core(inverse(r) * scale, 8)
        n = ROWS // (CORE * 8)
        mine_o[pl.ds(i * n, n), 16:] = own
        send_o[pl.ds(i * n, n), 16:] = other

    each(length, filter_step)


def transforms(place, slices, tables_v, thin, late, early, early_own, early_far):
    length = tables_v[0].shape[0]
    block = length // (X * YL)
    part = thin[0].shape[4] * 2 // 3
    features = late[0].shape[2] + early[0].shape[1]
    away = pl.BlockSpec(memory_space=pl.ANY)
    near = pl.BlockSpec(memory_space=pltpu.VMEM)
    shape = jax.ShapeDtypeStruct
    own = features // (CORE * 16)
    wave = pltpu.VMEM((length, part), F32)
    narrow = pltpu.VMEM((length, part), BF16)
    table = pltpu.VMEM((length, length), BF16)
    operands = (slices, *tables_v, *thin, *late, *early, early_own, early_far)
    return pl.pallas_call(
        transforms_body,
        out_shape=[shape((X * YL, block, 2 * part), BF16)] + [shape((own, 24, part), F32)] * 2,
        in_specs=[pl.BlockSpec(memory_space=pltpu.SMEM)] + [away] * len(operands),
        out_specs=[near] * 3,
        scratch_shapes=[
            pltpu.VMEM((X, YL, block, features), BF16),
            pltpu.VMEM((X * YL, block, part), BF16),
            pltpu.VMEM((X * YL, Z, YH, CORE, 16, part), BF16),
            pltpu.VMEM((X * YL, Z, YH, 16, part), BF16),
            *[table] * 4,
            *[wave] * 6,
            *[narrow] * 3,
            pltpu.SemaphoreType.DMA((48,)),
        ],
        compiler_params=pltpu.CompilerParams(vmem_limit_bytes=48 * 2**20),
        name="transforms",
    )(place, *operands)


def outputs_body(place, back, gates, upstream, *refs):
    pieces, (mixed_o, gate_o, input_o, w_v, grad_v, sem) = refs[:14], refs[14:]
    groups, block, _ = back.shape
    part = back.shape[2] // 2
    z, core = place[2], place[3]
    copies = []
    for n, c in ((0, core), (1, 1 - core)):
        for ref, (k, side) in zip(pieces[7 * n : 7 * n + 7], WIDE):
            some = pl.ds(0, groups) if side is None else pl.ds(side * groups // 2, groups // 2)
            to = lax.rem(z + k, Z)
            copies.append(pltpu.make_async_copy(ref, w_v.at[some, to, :, c], sem.at[len(copies)]))
    for copy in copies:
        copy.start()
    for g in range(groups):
        c = pl.ds(g * part, part)
        conv = back[g, :, :part].astype(F32)
        mixed_o[:, c] = (gates[:, c].astype(F32) * conv).astype(BF16)
        gate_o[:, c] = (upstream[:, c].astype(F32) * conv).astype(BF16)
        grad_v[:, c] = back[g, :, part:]
    for copy in copies:
        copy.wait()
    rows = w_v.shape[4]
    for g in range(groups):
        w = w_v[g].reshape(Z * YH * CORE * rows, w_v.shape[5])
        n = w.shape[0]
        y = lax.dot_general(grad_v[...], w, (((1,), (1,)), ((), ())), preferred_element_type=F32)
        input_o[:, pl.ds(g * n, n)] = y.astype(BF16)


def outputs(place, back, gates, upstream, pieces):
    groups, block, _ = back.shape
    channels = gates.shape[1]
    rows = pieces[0].shape[2]
    features = groups * Z * YH * CORE * rows
    away = pl.BlockSpec(memory_space=pl.ANY)
    near = pl.BlockSpec(memory_space=pltpu.VMEM)
    shape = jax.ShapeDtypeStruct
    return pl.pallas_call(
        outputs_body,
        out_shape=[shape((block, channels), BF16)] * 2 + [shape((block, features), BF16)],
        in_specs=[pl.BlockSpec(memory_space=pltpu.SMEM)] + [near] * 3 + [away] * 14,
        out_specs=[near] * 3,
        scratch_shapes=[
            pltpu.VMEM((groups, Z, YH, CORE, rows, channels), BF16),
            pltpu.VMEM((block, channels), BF16),
            pltpu.SemaphoreType.DMA((14,)),
        ],
        compiler_params=pltpu.CompilerParams(vmem_limit_bytes=32 * 2**20),
        name="outputs",
    )(place, back, gates, upstream, *pieces)


def local(activations, gate_values, in_weight, long_filter, out_cotangent):
    tokens = activations[0]
    gates = gate_values[0]
    upstream = out_cotangent[0]
    groups = X * YL
    replicas = Z * YH * CORE
    block, channels = gates.shape
    features = tokens.shape[1]
    length = block * groups
    part = channels // groups
    rows = in_weight.shape[0]
    shared = rows
    half = part // CORE
    cut = features * 5 // 8
    xi, yi, zi, hi, ci = (lax.axis_index(a) for a in SEQ + REP)
    place = jnp.stack([xi, yi, zi, ci])

    cosine, sine = (jnp.asarray(t.astype(np.float32)).astype(BF16) for t in tables(length))
    cosine_t, sine_t = (jnp.asarray(t.T.astype(np.float32)).astype(BF16) for t in tables(length))

    own_taps = lax.dynamic_slice_in_dim(long_filter, (zi * YH + hi) * shared, shared, 0)
    own_taps = pick(own_taps.reshape(shared, groups, CORE, half), ci, 2).reshape(shared, groups * half)
    piece = jnp.concatenate([in_weight, own_taps], axis=1)
    piece = in_order(piece, swap(piece, "yh"), hi).reshape(YH * rows, channels + groups * half)
    inner = (upstream.astype(F32) * gates.astype(F32)).astype(BF16)
    inner = inner.reshape(block // (YH * rows), YH * rows, groups, part).transpose(2, 1, 0, 3)
    early = tokens[:, cut:]
    early_lower, early_upper = up(early, "x"), down(early, "x")
    late_other = swap(tokens[:, :cut], "yl")
    sent = jnp.concatenate(
        [
            jnp.broadcast_to(piece[:, :channels], (groups, YH * rows, channels)),
            piece[:, channels:].reshape(YH * rows, groups, half).transpose(1, 0, 2),
            inner.reshape(groups, YH * rows, -1),
        ],
        axis=2,
    )
    sent = after(sent, early_lower, early_upper, late_other)
    slices = lax.all_to_all(sent, SEQ, 0, 0, tiled=True)
    late = in_order(tokens[:, :cut], late_other, yi)
    late_lower, late_upper = up(late, "x"), down(late, "x")
    n = block // 2
    early_far = (up(early_lower[:n], "x"), down(early_upper[n:], "x"))
    early_own = swap(jnp.stack([early, early_upper, early_lower]), "yl")
    early = (early, early_upper, early_lower, *early_far)
    slices = after(slices, late_lower, late_upper, *early_far, early_own)
    late = (late, late_upper, late_lower, up(late_lower[:1], "x"), down(late_upper[1:], "x"))
    early_far = swap(jnp.stack(early_far), "yl")

    thin = jnp.concatenate(
        [
            lax.dynamic_slice_in_dim(slices, (xi * YL + yi) * part, part, 2),
            slices[:, :, channels : channels + half],
        ],
        axis=2,
    ).reshape(groups, YH, rows, part + half)
    thin = halves_round(jnp.stack([thin, swap(thin, "core")]), "z")
    wide = slices[:, :, :channels].reshape(groups, YH, rows, channels)
    n = groups // 2
    first = (up(wide[:n], "z"), down(wide[n:], "z"))
    thin = (after(thin[0], *first), *thin[1:])
    second = (up(wide[n:], "z"), down(wide[:n], "z"))
    wide = (wide, second[1], first[1], first[0], second[0], up(first[0], "z"), down(first[1], "z"))
    wide = wide + tuple(swap(w, "core") for w in wide)

    pair, mine, other = transforms(
        place, slices, (cosine, sine, cosine_t, sine_t), thin, late, early, early_own, early_far
    )

    back = lax.all_to_all(pair, SEQ, 0, 0, tiled=True)
    owned = (mine + swap(other, "core")).astype(BF16)
    owned = lax.all_to_all(owned, SEQ + ("z", "yh"), 0, 0, tiled=True)
    owned = jnp.sum(owned.reshape(groups, Z * YH, -1, part).astype(F32), axis=1)
    owned = owned.transpose(1, 0, 2).reshape(-1, channels)

    mixed_out, gate_grad, input_grad = outputs(place, back, gates, upstream, wide)
    return (mixed_out[None], gate_grad[None], input_grad[None], owned[:rows], owned[rows:])


def solution(mesh):
    mesh = Mesh(mesh.devices.reshape(X, YL, Z, YH, CORE), SEQ + REP)
    split = P(REP, SEQ, None)
    in_specs = (split, split, P(SEQ + REP, None), P(SEQ, None), split)
    out_specs = (split, split, split, P(SEQ + REP, None), P(SEQ + REP, None))
    return jax.shard_map(local, mesh=mesh, in_specs=in_specs, out_specs=out_specs, check_vma=False)
```
